512 devices in a mesh: cuts: 4 (over x), dev: 128 (over z, y, core).
Axes of the slice: x: 4, y: 8, z: 8, core: 2. Of those that a mesh axis runs over, the one named last changes fastest.
Arguments:
- kv_cache: bfloat16 [4096, 128, 2048], P(('cuts', 'dev')), may hold values from -6 to 6
- queries: bfloat16 [4, 128, 768, 128], P('cuts', 'dev'), may hold values from -6 to 6
- gates: bfloat16 [4, 16, 768, 1024], P('cuts', None, 'dev'), may hold values from -6 to 6
- tokens: bfloat16 [4, 16, 768, 1024], P('cuts', None, 'dev'), may hold values from -6 to 6
- w_out: bfloat16 [1024, 1024], P('dev'), may hold values from -0.1875 to 0.1875
- norm_gain: float32 [1024], replicated, may hold values from 0.1 to 1.9
- hist_blocks: int32 [4, 64], replicated, may hold values from 1 to 32, as said below
- ranker_list: int32 [4, 64], replicated, may hold values from 0 to 63, as said below
- owner_ids: int32 [4, 64, 32], replicated, may hold values from -1 to 511, as said below
- slot_ids: int32 [4, 64, 32], replicated, may hold values from -1 to 7, as said below
- block_mask: int32 [4, 64, 6, 32], replicated, may hold values 0 or 1
Outputs:
- mixed: bfloat16 [4, 16, 768, 1024], P('cuts', None, 'dev')
The draws below stay inside these ranges and needn't reach their ends.
Inputs may be any that keep to these rules, and one draw needn't show every extreme that they name: `hist_blocks`: the entries of one slice sum to 1024, and one request of each slice has exactly 32 blocks. `ranker_list`: each slice's row is a permutation of its 64 requests. `owner_ids`: an entry is the cut index times 128 plus the dev index of the device that holds the block, and -1 exactly where b >= hist_blocks. Every device holds exactly 2 blocks of each slice's requests. The blocks of the 4 requests of one ranker group lie on devices of one dev index (over all cuts) at most 1 times, and some group reaches 1. `slot_ids`: -1 exactly where owner_ids is -1; the blocks of all slices use every cache row of every device exactly once.
All inputs are finite; a program needn't handle non-finite values.
Results may differ from the reference program's by a relative error of at most 0.0046.
Values may be sent and summed in bfloat16 or wider, within the bound.
No kernel may reach another device: no remote copies, remote signals or barrier semaphores. Data moves between devices by JAX's collectives and lax.ppermute only.
A program may use at most 128 MiB of HBM per device.

```python
import jax
import jax.numpy as jnp
from jax import lax

D = 1024
H = 8
DH = 128
BLK = 128
HB = 32
RQ = 4
CAND = 192
TILE = 32
OWN = 2
HD = 1024
GROUPS = 16
REQ_CUT = 64
ROWS_G = 768
CT = 6
BLOCKS = 4096
N_CUTS = 4
N_DEV = 128


def history_tables(key):
    requests = N_DEV // H * RQ
    live_total = OWN * N_CUTS * N_DEV
    cycle = N_CUTS * N_DEV
    pool_size = OWN * N_CUTS
    other_entries = requests - 1
    leftover_rows = live_total - HB - other_entries
    base_share = leftover_rows // other_entries
    extra_count = leftover_rows - base_share * other_entries
    key_cuts, key_rows = jax.random.split(key)

    def one_cut(cut_key, cut_index):
        key_spread, key_order, key_top, key_rank, key_offset, key_devs = jax.random.split(cut_key, 6)
        spread_rows = jax.random.randint(key_spread, (other_entries,), 0, base_share + 1)
        rank_order = jax.random.permutation(key_order, other_entries)
        extra_share = (rank_order < extra_count).astype(jnp.int32)
        remainder = 1 + base_share + extra_share + spread_rows - jnp.roll(spread_rows, 1)
        chosen = jax.random.randint(key_top, (), 0, requests)
        positions = jnp.arange(requests, dtype=jnp.int32)
        source = jnp.clip(positions - (positions > chosen).astype(jnp.int32), 0, other_entries - 1)
        lengths = jnp.where(positions == chosen, HB, remainder[source]).astype(jnp.int32)
        ranking = jax.random.permutation(key_rank, requests).astype(jnp.int32)
        ordered_length = lengths[ranking]
        is_live = (jnp.arange(HB, dtype=jnp.int32)[None, :] < ordered_length[:, None]).reshape(-1)
        counter = jnp.cumsum(is_live.astype(jnp.int32)) - 1
        offset = jax.random.randint(key_offset, (), 0, cycle)
        spot = (counter + offset) % live_total
        owner_flat = spot % cycle
        round_index = spot // cycle
        dev_order = jax.random.permutation(key_devs, N_DEV).astype(jnp.int32)
        owner_id = owner_flat // N_DEV * N_DEV + dev_order[owner_flat % N_DEV]
        local_row = cut_index * OWN + round_index
        return (lengths, ranking, owner_id, local_row, is_live)
    lengths, ranking, owner_rank, local_rank, live_rank = jax.vmap(one_cut)(jax.random.split(key_cuts, N_CUTS), jnp.arange(N_CUTS, dtype=jnp.int32))
    shuffles = jax.vmap(lambda owner: jax.random.permutation(jax.random.fold_in(key_rows, owner), pool_size))(jnp.arange(cycle, dtype=jnp.int32)).astype(jnp.int32)
    slot_rank = shuffles[jnp.clip(owner_rank, 0, cycle - 1), local_rank]
    owner_rank = jnp.where(live_rank, owner_rank, -1)
    slot_rank = jnp.where(live_rank, slot_rank, -1)
    inverse = jnp.argsort(ranking, axis=1)
    cut_rows = jnp.arange(N_CUTS)[:, None]
    owners = owner_rank.reshape(N_CUTS, requests, HB)[cut_rows, inverse]
    slots = slot_rank.reshape(N_CUTS, requests, HB)[cut_rows, inverse]
    return (lengths, ranking, owners.astype(jnp.int32), slots.astype(jnp.int32))


def draw_hist_blocks(key, part):
    return history_tables(key)[0]


def draw_ranker_list(key, part):
    return history_tables(key)[1]


def draw_owner_ids(key, part):
    return history_tables(key)[2]


def draw_slot_ids(key, part):
    return history_tables(key)[3]


def set_ends(result, rng, low, high):
    index_at = [jax.random.randint(jax.random.fold_in(rng, axis), (), 0, length) for axis, length in enumerate(result.shape)]
    main_axis = result.shape.index(max(result.shape))
    next_to = index_at[:main_axis] + [(index_at[main_axis] + 1) % result.shape[main_axis]] + index_at[main_axis + 1:]
    return result.at[tuple(index_at)].set(low).at[tuple(next_to)].set(high)


def steps_of(rng, extent, pieces, smallest, high):
    loudness, own = 1.0, jax.random.fold_in(rng, 6)
    for dim, parts in pieces:
        draws = jnp.exp(jax.random.uniform(jax.random.fold_in(own, dim), (parts,), jnp.float32, smallest / len(pieces), high / len(pieces)))
        loudness = loudness * jnp.repeat(draws, extent[dim] // parts).reshape([-1 if axis == dim else 1 for axis in range(len(extent))])
    return loudness


def gaussian(own_key, extent, width, limit, cuts=(), kind=jnp.bfloat16):
    result = width * jax.random.normal(own_key, extent, jnp.float32)
    if cuts:
        result = result * steps_of(own_key, extent, cuts, -0.22, 0.18)
    return jnp.clip(result, -limit, limit).astype(kind)


def setup_inputs(seed: int = 0) -> dict:
    key_of = jax.random.split(jax.random.key(seed), 12)
    kv_cache = gaussian(key_of[0], (BLOCKS, BLK, 2 * HD), 1.0, 6.0, ((0, 512),))
    queries = gaussian(key_of[1], (N_CUTS, N_DEV, ROWS_G, DH), 1.0, 6.0, ((0, 4), (1, 128)))
    gates = gaussian(key_of[2], (N_CUTS, GROUPS, ROWS_G, HD), 1.0, 6.0, ((0, 4), (2, 128)))
    tokens = gaussian(key_of[3], (N_CUTS, GROUPS, ROWS_G, D), 1.0, 6.0, ((0, 4), (2, 128)))
    w_out = gaussian(key_of[4], (HD, D), HD ** -0.5, 0.1875, ((0, 128),))
    norm_gain = jnp.clip(1.0 + 0.18 * jax.random.normal(key_of[5], (HD,), jnp.float32), 0.1, 1.9)
    hist_blocks = draw_hist_blocks(jax.random.fold_in(key_of[11], 71), 0)
    ranker_list = draw_ranker_list(jax.random.fold_in(key_of[11], 71), 0)
    owner_ids = draw_owner_ids(jax.random.fold_in(key_of[11], 71), 0)
    slot_ids = draw_slot_ids(jax.random.fold_in(key_of[11], 71), 0)
    block_mask = set_ends((jax.random.randint(key_of[10], (N_CUTS, REQ_CUT, CT, HB), 0, 4) < 3).astype(jnp.int32), jax.random.fold_in(key_of[10], 1), 0, 1)
    return dict(kv_cache=kv_cache, queries=queries, gates=gates, tokens=tokens, w_out=w_out, norm_gain=norm_gain, hist_blocks=hist_blocks, ranker_list=ranker_list, owner_ids=owner_ids, slot_ids=slot_ids, block_mask=block_mask)


EPS = 1e-05

def attend_request(query, blocks, allowed):
    key_rows = blocks[:, :, :, 0, :].astype(jnp.float32)
    value_rows = blocks[:, :, :, 1, :].astype(jnp.float32)
    scores = jnp.einsum('hce,bkhe->hcbk', query.astype(jnp.float32), key_rows) * DH ** (-0.5)
    weights = (jax.nn.silu(scores) * allowed[None, :, :, None]).astype(jnp.bfloat16)
    attended = jnp.einsum('hcbk,bkhe->che', weights.astype(jnp.float32), value_rows)
    return attended.astype(jnp.bfloat16)

def reference(kv_cache, queries, gates, tokens, w_out, norm_gain, hist_blocks, ranker_list, owner_ids, slot_ids, block_mask):
    groups = N_DEV // H
    pool_size = OWN * N_CUTS
    cache_blocks = kv_cache.reshape(-1, BLK, H, 2, DH)
    query_heads = queries.reshape(N_CUTS, H, groups, RQ, CAND, DH)

    def one_request(flat_index):
        cut_index = flat_index // (groups * RQ)
        within = flat_index % (groups * RQ)
        group_index = within // RQ
        slot_index = within % RQ
        request = ranker_list[cut_index, group_index * RQ + slot_index]
        length = hist_blocks[cut_index, request]
        rows = owner_ids[cut_index, request] * pool_size + slot_ids[cut_index, request]
        blocks = cache_blocks[jnp.maximum(rows, 0)]
        is_live = (jnp.arange(HB, dtype=jnp.int32) < length).astype(jnp.int32)
        tile_mask = block_mask[cut_index, request] * is_live[None, :]
        allowed = jnp.repeat(tile_mask, TILE, axis=0).astype(jnp.float32)
        query = query_heads[cut_index, :, group_index, slot_index]
        return attend_request(query, blocks, allowed)
    attended = lax.map(one_request, jnp.arange(N_CUTS * groups * RQ, dtype=jnp.int32))
    attended = attended.reshape(N_CUTS, groups, RQ * CAND, H * DH).astype(jnp.float32)
    row_mean = lax.optimization_barrier(jnp.mean(attended, axis=-1, keepdims=True))
    centred = attended - row_mean
    variance = lax.optimization_barrier(jnp.mean(centred * centred, axis=-1, keepdims=True))
    normed = centred * lax.rsqrt(variance + EPS) * norm_gain.astype(jnp.float32)
    gated = (normed * jax.nn.silu(gates.astype(jnp.float32))).astype(jnp.bfloat16)
    projected = jnp.dot(gated.reshape(-1, H * DH), w_out, preferred_element_type=jnp.float32)
    projected = projected.reshape(N_CUTS, groups, RQ * CAND, D)
    return (tokens.astype(jnp.float32) + projected).astype(jnp.bfloat16)
```

```python
import jax
import jax.numpy as jnp
from jax import lax
from jax.experimental import pallas as pl
from jax.experimental.pallas import tpu as pltpu
from jax.sharding import Mesh, PartitionSpec as P

H = 8
DH = 128
HB = 32
RQ = 4
TILE = 32
BLK = 128
CUTS, ZS, YS, CORES = 4, 8, 8, 2
GROUPS = 16
REQUESTS = 64
CAND = 192
CT = 6
ROWS_G = RQ * CAND
OWN = 2
SLAB = 2 * DH
PIECE = 6
SOURCES = CUTS * ZS
BLOCKS_HERE = SOURCES * OWN
KV_STEP = 8
EPS = 1e-05


def pack_kernel(self_ref, owner_ref, slot_ref, kv_ref, out_ref, held, in_sems, out_sems):
    me = self_ref[0]
    rows = lax.broadcasted_iota(jnp.int32, (REQUESTS, HB), 0)
    blocks = lax.broadcasted_iota(jnp.int32, (REQUESTS, HB), 1)
    place = (rows * HB + blocks) * 8
    fetches = []
    for cut in range(CUTS):
        mine = owner_ref[cut] == me
        code = place + slot_ref[cut]
        first = jnp.min(jnp.where(mine, code, REQUESTS * HB * 8 - 1))
        last = jnp.max(jnp.where(mine, code, 0))
        for own, found in enumerate((first, last)):
            i = cut * OWN + own
            fetch = pltpu.make_async_copy(kv_ref.at[found & 7], held.at[i], in_sems.at[i])
            fetch.start()
            fetches.append(fetch)
    stores = []
    for i, fetch in enumerate(fetches):
        fetch.wait()
        for head in range(H):
            store = pltpu.make_async_copy(
                held.at[i, :, pl.ds(head * SLAB, SLAB)],
                out_ref.at[(i // OWN) * H + head, i % OWN],
                out_sems.at[i * H + head],
            )
            store.start()
            stores.append(store)
    for store in stores:
        store.wait()


def pack(me, owner_ids, slot_ids, kv_cache):
    count = CUTS * OWN
    return pl.pallas_call(
        pack_kernel,
        out_shape=jax.ShapeDtypeStruct((SOURCES, OWN, BLK, SLAB), kv_cache.dtype),
        in_specs=[
            pl.BlockSpec(memory_space=pltpu.SMEM),
            pl.BlockSpec(memory_space=pltpu.VMEM),
            pl.BlockSpec(memory_space=pltpu.VMEM),
            pl.BlockSpec(memory_space=pl.ANY),
        ],
        out_specs=pl.BlockSpec(memory_space=pl.ANY),
        scratch_shapes=[
            pltpu.VMEM((count, BLK, H * SLAB), kv_cache.dtype),
            pltpu.SemaphoreType.DMA((count,)),
            pltpu.SemaphoreType.DMA((count * H,)),
        ],
        compiler_params=pltpu.CompilerParams(vmem_limit_bytes=24 << 20),
    )(me.reshape(1), owner_ids, slot_ids, kv_cache)


def attend_kernel(pos_ref, core_ref, mask_ref, q_ref, kv_ref, keep_ref, send_ref, acc_ref):
    step = pl.program_id(0)

    @pl.when(step == 0)
    def _():
        def clear(i, carry):
            acc_ref[pl.ds(pl.multiple_of(i * CAND, CAND), CAND), :] = jnp.zeros((CAND, DH), jnp.float32)
            return carry

        lax.fori_loop(0, REQUESTS, clear, 0)

    for u in range(KV_STEP):
        block = step * KV_STEP + u
        rows = pl.ds(pl.multiple_of(pos_ref[block] * CAND, CAND), CAND)
        query = q_ref[rows, :]
        scores = lax.dot_general(
            query, kv_ref[u, :, :DH], (((1,), (1,)), ((), ())), preferred_element_type=jnp.float32
        )
        half = scores * (0.5 * DH ** (-0.5))
        silu = half + half * jnp.tanh(half)
        weights = jnp.concatenate(
            [
                (silu[t * TILE : (t + 1) * TILE] * mask_ref[block * CT + t]).astype(jnp.bfloat16)
                for t in range(CT)
            ],
            axis=0,
        )
        acc_ref[rows, :] += jnp.dot(weights, kv_ref[u, :, DH:], preferred_element_type=jnp.float32)

    @pl.when(step == BLOCKS_HERE // KV_STEP - 1)
    def _():
        core = core_ref[0]

        def split(target, carry):
            base = target * (CORES * PIECE)
            for r in range(PIECE):
                for ref, side in ((keep_ref, core), (send_ref, 1 - core)):
                    first = base + side * PIECE + r
                    ref[target, pl.ds(r * GROUPS, GROUPS), :] = acc_ref[
                        pl.ds(first, GROUPS, stride=ROWS_G), :
                    ].astype(ref.dtype)
            return carry

        lax.fori_loop(0, ZS * YS, split, 0)


def attend(positions, core, masks, queries, blocks):
    piece = jax.ShapeDtypeStruct((ZS * YS, GROUPS * PIECE, DH), jnp.bfloat16)
    whole = pl.BlockSpec((ZS * YS, GROUPS * PIECE, DH), lambda i, *_: (0, 0, 0))
    flops = 4 * BLOCKS_HERE * CAND * BLK * DH
    return pl.pallas_call(
        attend_kernel,
        out_shape=(piece, piece),
        grid_spec=pltpu.PrefetchScalarGridSpec(
            num_scalar_prefetch=3,
            grid=(BLOCKS_HERE // KV_STEP,),
            in_specs=[
                pl.BlockSpec((REQUESTS * CAND, DH), lambda i, *_: (0, 0)),
                pl.BlockSpec((KV_STEP, BLK, SLAB), lambda i, *_: (i, 0, 0)),
            ],
            out_specs=(whole, whole),
            scratch_shapes=[pltpu.VMEM((REQUESTS * CAND, DH), jnp.float32)],
        ),
        compiler_params=pltpu.CompilerParams(
            vmem_limit_bytes=40 << 20, dimension_semantics=("arbitrary",)
        ),
        cost_estimate=pl.CostEstimate(
            flops=flops, bytes_accessed=10 << 20, transcendentals=BLOCKS_HERE * CAND * BLK
        ),
    )(positions, core, masks, queries, blocks)


def finish_kernel(back_ref, gain_ref, gate_ref, token_ref, w_ref, out_ref):
    heads = []
    for head in range(H):
        total = back_ref[head * YS].astype(jnp.float32)
        for y in range(1, YS):
            total = total + back_ref[head * YS + y].astype(jnp.float32)
        heads.append(total.astype(jnp.bfloat16).astype(jnp.float32))
    rows = jnp.concatenate(heads, axis=1)
    centred = rows - jnp.mean(rows, axis=-1, keepdims=True)
    variance = jnp.mean(centred * centred, axis=-1, keepdims=True)
    normed = centred * lax.rsqrt(variance + EPS) * gain_ref[...]
    gate = gate_ref[...].astype(jnp.float32)
    gated = (normed * (gate * jax.nn.sigmoid(gate))).astype(jnp.bfloat16)
    projected = jnp.dot(gated, w_ref[...], preferred_element_type=jnp.float32)
    out_ref[...] = (token_ref[...].astype(jnp.float32) + projected).astype(out_ref.dtype)


def finish(back, gain, gate_rows, token_rows, w_all):
    return pl.pallas_call(
        finish_kernel,
        out_shape=jax.ShapeDtypeStruct(token_rows.shape, token_rows.dtype),
        in_specs=[pl.BlockSpec(memory_space=pltpu.VMEM)] * 5,
        out_specs=pl.BlockSpec(memory_space=pltpu.VMEM),
        compiler_params=pltpu.CompilerParams(vmem_limit_bytes=24 << 20),
    )(back, gain, gate_rows, token_rows, w_all)


def describe(cut, yc, hist_blocks, ranker_list, owner_ids, block_mask):
    owners = lax.dynamic_index_in_dim(owner_ids, cut, 0, keepdims=False).reshape(-1)
    ranking = lax.dynamic_index_in_dim(ranker_list, cut, 0, keepdims=False)
    lengths = lax.dynamic_index_in_dim(hist_blocks, cut, 0, keepdims=False)
    tiles = lax.dynamic_index_in_dim(block_mask, cut, 0, keepdims=False)
    source = jnp.arange(SOURCES, dtype=jnp.int32)
    source = (source // ZS) * (ZS * YS * CORES) + (source % ZS) * (YS * CORES) + yc
    found = owners[None, :] == source[:, None]
    place = jnp.arange(REQUESTS * HB, dtype=jnp.int32)[None, :]
    first = jnp.min(jnp.where(found, place, REQUESTS * HB - 1), axis=1)
    last = jnp.max(jnp.where(found, place, 0), axis=1)
    places = jnp.stack([first, last], axis=1).reshape(-1)
    request, block = places // HB, places % HB
    slots = jnp.arange(REQUESTS, dtype=jnp.int32)
    positions = jnp.sum(jnp.where(ranking[None, :] == request[:, None], slots[None, :], 0), axis=1)
    live = (block < lengths[request]).astype(jnp.float32)
    masks = tiles[request, :, block].astype(jnp.float32) * live[:, None]
    return positions, masks.reshape(-1)


def local(
    kv_cache,
    queries,
    gates,
    tokens,
    w_out,
    norm_gain,
    hist_blocks,
    ranker_list,
    owner_ids,
    slot_ids,
    block_mask,
):
    cut = lax.axis_index("cuts")
    core = lax.axis_index("core")
    me = lax.axis_index(("cuts", "z", "y", "core"))
    yc = lax.axis_index(("y", "core"))
    packed = pack(me, owner_ids, slot_ids, kv_cache)
    arrived = lax.all_to_all(packed, ("cuts", "z"), split_axis=0, concat_axis=0, tiled=True)
    query_all = lax.all_gather(queries.reshape(ROWS_G, DH), ("y", "core"), axis=0, tiled=True)
    w_all = lax.all_gather(w_out, ("z", "y", "core"), axis=0, tiled=True)
    positions, masks = describe(cut, yc, hist_blocks, ranker_list, owner_ids, block_mask)
    keep, send = attend(
        positions, core.reshape(1), masks, query_all, arrived.reshape(BLOCKS_HERE, BLK, SLAB)
    )
    other = lax.ppermute(send, "core", [(0, 1), (1, 0)])
    both = (keep.astype(jnp.float32) + other.astype(jnp.float32)).astype(jnp.bfloat16)
    back = lax.all_to_all(both, ("z", "y"), split_axis=0, concat_axis=0, tiled=True)
    width = H * DH
    gate_rows = gates.reshape(GROUPS, PIECE, width).transpose(1, 0, 2).reshape(-1, width)
    token_rows = tokens.reshape(GROUPS, PIECE, width).transpose(1, 0, 2).reshape(-1, width)
    mixed = finish(back, norm_gain.reshape(1, width), gate_rows, token_rows, w_all)
    return mixed.reshape(PIECE, GROUPS, width).transpose(1, 0, 2).reshape(tokens.shape)


def solution(mesh):
    grid = Mesh(
        mesh.devices.reshape(CUTS, ZS, YS, CORES), ("cuts", "z", "y", "core")
    )
    dev = ("z", "y", "core")
    return jax.shard_map(
        local,
        mesh=grid,
        in_specs=(
            P(("cuts",) + dev, None, None),
            P("cuts", dev, None, None),
            P("cuts", None, dev, None),
            P("cuts", None, dev, None),
            P(dev, None),
            P(),
            P(),
            P(),
            P(),
            P(),
            P(),
        ),
        out_specs=P("cuts", None, dev, None),
        check_vma=False,
    )
```

```python
import jax
import jax.numpy as jnp
from jax import lax
from jax.experimental import pallas as pl
from jax.experimental.pallas import tpu as pltpu
from jax.sharding import Mesh, PartitionSpec as P

H = 8
DH = 128
HB = 32
RQ = 4
TILE = 32
BLK = 128
CUTS, ZS, YS, CORES = 4, 8, 8, 2
GROUPS = 16
REQUESTS = 64
CAND = 192
CT = 6
ROWS_G = RQ * CAND
OWN = 2
SLAB = 2 * DH
PIECE = 6
SOURCES = CUTS * ZS
BLOCKS_HERE = SOURCES * OWN
KV_STEP = 8
EPS = 1e-05
W_ROWS = 64
PAYLOAD = ROWS_G + W_ROWS


def pack_kernel(self_ref, owner_hbm, slot_hbm, kv_ref, out_ref, owner_ref, slot_ref, held, sems, in_sems, out_sems):
    me = self_ref[0]
    tables = [
        pltpu.make_async_copy(owner_hbm, owner_ref, sems.at[0]),
        pltpu.make_async_copy(slot_hbm, slot_ref, sems.at[1]),
    ]
    for table in tables:
        table.start()
    for table in tables:
        table.wait()
    blocks = lax.broadcasted_iota(jnp.int32, (HB, REQUESTS), 0)
    rows = lax.broadcasted_iota(jnp.int32, (HB, REQUESTS), 1)
    place = (rows * HB + blocks) * 8
    fetches = []
    for cut in range(CUTS):
        mine = owner_ref[cut] == me
        code = place + slot_ref[cut]
        first = jnp.min(jnp.where(mine, code, REQUESTS * HB * 8 - 1))
        last = jnp.max(jnp.where(mine, code, 0))
        for own, found in enumerate((first, last)):
            i = cut * OWN + own
            fetch = pltpu.make_async_copy(kv_ref.at[found & 7], held.at[i], in_sems.at[i])
            fetch.start()
            fetches.append(fetch)
    stores = []
    for i, fetch in enumerate(fetches):
        fetch.wait()
        for head in range(H):
            store = pltpu.make_async_copy(
                held.at[i, :, pl.ds(head * SLAB, SLAB)],
                out_ref.at[(i // OWN) * H + head, i % OWN],
                out_sems.at[i * H + head],
            )
            store.start()
            stores.append(store)
    for store in stores:
        store.wait()


def pack(me, owner_ids, slot_ids, kv_cache):
    count = CUTS * OWN
    owner_ids, slot_ids = owner_ids.transpose(0, 2, 1), slot_ids.transpose(0, 2, 1)
    return pl.pallas_call(
        pack_kernel,
        out_shape=jax.ShapeDtypeStruct((SOURCES, OWN, BLK, SLAB), kv_cache.dtype),
        in_specs=[
            pl.BlockSpec(memory_space=pltpu.SMEM),
            pl.BlockSpec(memory_space=pltpu.HBM),
            pl.BlockSpec(memory_space=pltpu.HBM),
            pl.BlockSpec(memory_space=pltpu.HBM),
        ],
        out_specs=pl.BlockSpec(memory_space=pltpu.HBM),
        scratch_shapes=[
            pltpu.VMEM(owner_ids.shape, jnp.int32),
            pltpu.VMEM(slot_ids.shape, jnp.int32),
            pltpu.VMEM((count, BLK, H * SLAB), kv_cache.dtype),
            pltpu.SemaphoreType.DMA((2,)),
            pltpu.SemaphoreType.DMA((count,)),
            pltpu.SemaphoreType.DMA((count * H,)),
        ],
        compiler_params=pltpu.CompilerParams(vmem_limit_bytes=60 << 20),
    )(me.reshape(1), owner_ids, slot_ids, kv_cache)


def attend_kernel(
    pos_ref, core_ref, mask_ref, q_hbm, kv_hbm, keep_hbm, send_hbm, q_ref, kv_ref, acc_ref, keep_ref, send_ref, q_sems, in_sems, out_sems
):
    steps = BLOCKS_HERE // KV_STEP

    def fetch(step):
        part = pl.ds(step * KV_STEP, KV_STEP)
        return pltpu.make_async_copy(kv_hbm.at[part], kv_ref.at[part], in_sems.at[step])

    asked = []
    for group in range(GROUPS):
        asked.append(pltpu.make_async_copy(q_hbm.at[group, pl.ds(0, ROWS_G)], q_ref.at[group], q_sems.at[group]))
        asked[-1].start()
    for step in range(steps):
        fetch(step).start()

    def clear(i, carry):
        acc_ref[pl.ds(pl.multiple_of(i * CAND, CAND), CAND), :] = jnp.zeros((CAND, DH), jnp.float32)
        return carry

    lax.fori_loop(0, REQUESTS, clear, 0, unroll=4)
    for copy in asked:
        copy.wait()

    def work(step, carry):
        fetch(step).wait()
        parts = []
        for u in range(KV_STEP):
            block = step * KV_STEP + u
            place = pos_ref[block]
            query = q_ref[place >> 2, pl.ds(pl.multiple_of((place & 3) * CAND, CAND), CAND), :]
            keys = kv_ref[block, :, :DH].astype(jnp.float32).T.astype(jnp.bfloat16)
            scores = jnp.dot(query, keys, preferred_element_type=jnp.float32)
            half = scores * (0.5 * DH ** (-0.5))
            silu = half + half * jnp.tanh(half)
            weights = jnp.concatenate(
                [
                    (silu[t * TILE : (t + 1) * TILE] * mask_ref[block * CT + t]).astype(jnp.bfloat16)
                    for t in range(CT)
                ],
                axis=0,
            )
            parts.append(jnp.dot(weights, kv_ref[block, :, DH:], preferred_element_type=jnp.float32))
        for u in range(KV_STEP):
            rows = pl.ds(pl.multiple_of(pos_ref[step * KV_STEP + u] * CAND, CAND), CAND)
            acc_ref[rows, :] += parts[u]
        return carry

    lax.fori_loop(0, steps, work, 0)

    core = core_ref[0]
    copies = []
    for out, (ref, hbm, side) in enumerate(((send_ref, send_hbm, 1 - core), (keep_ref, keep_hbm, core))):

        def split(target, carry):
            first = target * (CORES * PIECE) + side * PIECE
            for r in range(PIECE):
                ref[target, pl.ds(r * GROUPS, GROUPS), :] = acc_ref[
                    pl.ds(first + r, GROUPS, stride=ROWS_G), :
                ].astype(ref.dtype)
            return carry

        for z in range(0, ZS, 2):
            part = pl.ds(z * YS, 2 * YS)
            lax.fori_loop(z * YS, (z + 2) * YS, split, 0, unroll=4)
            copy = pltpu.make_async_copy(ref.at[part], hbm.at[part], out_sems.at[out * ZS + z])
            copy.start()
            copies.append(copy)
    for copy in copies:
        copy.wait()


def attend(positions, core, masks, payload, blocks):
    piece = jax.ShapeDtypeStruct((ZS * YS, GROUPS * PIECE, DH), jnp.bfloat16)
    smem, hbm = pl.BlockSpec(memory_space=pltpu.SMEM), pl.BlockSpec(memory_space=pltpu.HBM)
    return pl.pallas_call(
        attend_kernel,
        out_shape=(piece, piece),
        in_specs=[smem, smem, smem, hbm, hbm],
        out_specs=(hbm, hbm),
        scratch_shapes=[
            pltpu.VMEM((GROUPS, ROWS_G, DH), payload.dtype),
            pltpu.VMEM(blocks.shape, blocks.dtype),
            pltpu.VMEM((REQUESTS * CAND, DH), jnp.float32),
            pltpu.VMEM(piece.shape, piece.dtype),
            pltpu.VMEM(piece.shape, piece.dtype),
            pltpu.SemaphoreType.DMA((GROUPS,)),
            pltpu.SemaphoreType.DMA((BLOCKS_HERE // KV_STEP,)),
            pltpu.SemaphoreType.DMA((2 * ZS,)),
        ],
        compiler_params=pltpu.CompilerParams(vmem_limit_bytes=60 << 20),
        cost_estimate=pl.CostEstimate(
            flops=4 * BLOCKS_HERE * CAND * BLK * DH,
            bytes_accessed=10 << 20,
            transcendentals=BLOCKS_HERE * CAND * BLK,
        ),
    )(positions, core, masks, payload, blocks)


def finish_kernel(back_ref, gain_ref, gate_ref, token_ref, w_ref, out_ref):
    heads = []
    for head in range(H):
        total = back_ref[head * YS].astype(jnp.float32)
        for y in range(1, YS):
            total = total + back_ref[head * YS + y].astype(jnp.float32)
        heads.append(total.astype(jnp.bfloat16).astype(jnp.float32))
    rows = jnp.concatenate(heads, axis=1)
    centred = rows - jnp.mean(rows, axis=-1, keepdims=True)
    variance = jnp.mean(centred * centred, axis=-1, keepdims=True)
    normed = centred * lax.rsqrt(variance + EPS) * gain_ref[...]
    gate = gate_ref[...].astype(jnp.float32)
    gated = (normed * (gate * jax.nn.sigmoid(gate))).astype(jnp.bfloat16)
    projected = jnp.dot(gated, w_ref[...], preferred_element_type=jnp.float32)
    out_ref[...] = (token_ref[...].astype(jnp.float32) + projected).astype(out_ref.dtype)


def finish(back, gain, gate_rows, token_rows, w_all):
    return pl.pallas_call(
        finish_kernel,
        out_shape=jax.ShapeDtypeStruct(token_rows.shape, token_rows.dtype),
        in_specs=[pl.BlockSpec(memory_space=pltpu.VMEM)] * 5,
        out_specs=pl.BlockSpec(memory_space=pltpu.VMEM),
        compiler_params=pltpu.CompilerParams(vmem_limit_bytes=24 << 20),
    )(back, gain, gate_rows, token_rows, w_all)


def describe(cut, yc, hist_blocks, ranker_list, owner_ids, block_mask):
    owners = lax.dynamic_index_in_dim(owner_ids, cut, 0, keepdims=False).reshape(-1)
    ranking = lax.dynamic_index_in_dim(ranker_list, cut, 0, keepdims=False)
    lengths = lax.dynamic_index_in_dim(hist_blocks, cut, 0, keepdims=False)
    tiles = lax.dynamic_index_in_dim(block_mask, cut, 0, keepdims=False)
    source = jnp.arange(SOURCES, dtype=jnp.int32)
    source = (source // ZS) * (ZS * YS * CORES) + (source % ZS) * (YS * CORES) + yc
    found = owners[None, :] == source[:, None]
    place = jnp.arange(REQUESTS * HB, dtype=jnp.int32)[None, :]
    first = jnp.min(jnp.where(found, place, REQUESTS * HB - 1), axis=1)
    last = jnp.max(jnp.where(found, place, 0), axis=1)
    places = jnp.stack([first, last], axis=1).reshape(-1)
    request, block = places // HB, places % HB
    slots = jnp.arange(REQUESTS, dtype=jnp.int32)
    positions = jnp.sum(jnp.where(ranking[None, :] == request[:, None], slots[None, :], 0), axis=1)
    live = (block < lengths[request]).astype(jnp.float32)
    masks = tiles[request, :, block].astype(jnp.float32) * live[:, None]
    return positions, masks.reshape(-1)


def local(
    kv_cache,
    queries,
    gates,
    tokens,
    w_out,
    norm_gain,
    hist_blocks,
    ranker_list,
    owner_ids,
    slot_ids,
    block_mask,
):
    cut = lax.axis_index("cuts")
    core = lax.axis_index("core")
    me = lax.axis_index(("cuts", "z", "y", "core"))
    yc = lax.axis_index(("y", "core"))
    packed = pack(me, owner_ids, slot_ids, kv_cache)
    arrived = lax.all_to_all(packed, ("cuts", "z"), split_axis=0, concat_axis=0, tiled=True)
    payload = jnp.concatenate([queries.reshape(ROWS_G, DH), w_out.reshape(W_ROWS, DH)], axis=0)
    payload = lax.all_gather(payload, ("y", "core"), axis=0, tiled=True).reshape(GROUPS, PAYLOAD, DH)
    w_head = payload[:, ROWS_G:].reshape(DH, H * DH)
    w_all = lax.all_gather(w_head, "z", axis=0, tiled=True)
    positions, masks = describe(cut, yc, hist_blocks, ranker_list, owner_ids, block_mask)
    keep, send = attend(
        positions, core.reshape(1), masks, payload, arrived.reshape(BLOCKS_HERE, BLK, SLAB)
    )
    other = lax.ppermute(send, "core", [(0, 1), (1, 0)])
    both = (keep.astype(jnp.float32) + other.astype(jnp.float32)).astype(jnp.bfloat16)
    back = lax.all_to_all(both, ("z", "y"), split_axis=0, concat_axis=0, tiled=True)
    width = H * DH
    gate_rows = gates.reshape(GROUPS, PIECE, width).transpose(1, 0, 2).reshape(-1, width)
    token_rows = tokens.reshape(GROUPS, PIECE, width).transpose(1, 0, 2).reshape(-1, width)
    mixed = finish(back, norm_gain.reshape(1, width), gate_rows, token_rows, w_all)
    return mixed.reshape(PIECE, GROUPS, width).transpose(1, 0, 2).reshape(tokens.shape)


def solution(mesh):
    grid = Mesh(
        mesh.devices.reshape(CUTS, ZS, YS, CORES), ("cuts", "z", "y", "core")
    )
    dev = ("z", "y", "core")
    return jax.shard_map(
        local,
        mesh=grid,
        in_specs=(
            P(("cuts",) + dev, None, None),
            P("cuts", dev, None, None),
            P("cuts", None, dev, None),
            P("cuts", None, dev, None),
            P(dev, None),
            P(),
            P(),
            P(),
            P(),
            P(),
            P(),
        ),
        out_specs=P("cuts", None, dev, None),
        check_vma=False,
    )
```

```python
import jax
import jax.numpy as jnp
from jax import lax
from jax.experimental import pallas as pl
from jax.experimental.pallas import tpu as pltpu
from jax.sharding import Mesh, PartitionSpec as P

H = 8
DH = 128
HB = 32
RQ = 4
TILE = 32
BLK = 128
CUTS, ZS, YS, CORES = 4, 8, 8, 2
GROUPS = 16
REQUESTS = 64
CAND = 192
CT = 6
ROWS_G = RQ * CAND
OWN = 2
SLAB = 2 * DH
PIECE = 6
SOURCES = CUTS * ZS
BLOCKS_HERE = SOURCES * OWN
KV_STEP = 8
EPS = 1e-05


def pack_kernel(self_ref, owner_hbm, slot_hbm, kv_ref, out_ref, owner_ref, slot_ref, held, sems, in_sems, out_sems):
    me = self_ref[0]
    tables = [
        pltpu.make_async_copy(owner_hbm, owner_ref, sems.at[0]),
        pltpu.make_async_copy(slot_hbm, slot_ref, sems.at[1]),
    ]
    for table in tables:
        table.start()
    for table in tables:
        table.wait()
    blocks = lax.broadcasted_iota(jnp.int32, (HB, REQUESTS), 0)
    rows = lax.broadcasted_iota(jnp.int32, (HB, REQUESTS), 1)
    place = (rows * HB + blocks) * 8
    fetches = []
    for cut in range(CUTS):
        mine = owner_ref[cut] == me
        code = place + slot_ref[cut]
        first = jnp.min(jnp.where(mine, code, REQUESTS * HB * 8 - 1))
        last = jnp.max(jnp.where(mine, code, 0))
        for own, found in enumerate((first, last)):
            i = cut * OWN + own
            fetch = pltpu.make_async_copy(kv_ref.at[found & 7], held.at[i], in_sems.at[i])
            fetch.start()
            fetches.append(fetch)
    stores = []
    for i, fetch in enumerate(fetches):
        fetch.wait()
        for head in range(H):
            store = pltpu.make_async_copy(
                held.at[i, :, pl.ds(head * SLAB, SLAB)],
                out_ref.at[(i // OWN) * H + head, i % OWN],
                out_sems.at[i * H + head],
            )
            store.start()
            stores.append(store)
    for store in stores:
        store.wait()


def pack(me, owner_ids, slot_ids, kv_cache):
    count = CUTS * OWN
    owner_ids, slot_ids = owner_ids.transpose(0, 2, 1), slot_ids.transpose(0, 2, 1)
    return pl.pallas_call(
        pack_kernel,
        out_shape=jax.ShapeDtypeStruct((SOURCES, OWN, BLK, SLAB), kv_cache.dtype),
        in_specs=[
            pl.BlockSpec(memory_space=pltpu.SMEM),
            pl.BlockSpec(memory_space=pltpu.HBM),
            pl.BlockSpec(memory_space=pltpu.HBM),
            pl.BlockSpec(memory_space=pltpu.HBM),
        ],
        out_specs=pl.BlockSpec(memory_space=pltpu.HBM),
        scratch_shapes=[
            pltpu.VMEM(owner_ids.shape, jnp.int32),
            pltpu.VMEM(slot_ids.shape, jnp.int32),
            pltpu.VMEM((count, BLK, H * SLAB), kv_cache.dtype),
            pltpu.SemaphoreType.DMA((2,)),
            pltpu.SemaphoreType.DMA((count,)),
            pltpu.SemaphoreType.DMA((count * H,)),
        ],
        compiler_params=pltpu.CompilerParams(vmem_limit_bytes=60 << 20),
    )(me.reshape(1), owner_ids, slot_ids, kv_cache)


def attend_kernel(
    pos_ref, core_ref, mask_ref, q_hbm, kv_hbm, keep_hbm, send_hbm, q_ref, kv_ref, acc_ref, keep_ref, send_ref, q_sems, in_sems, out_sems
):
    steps = BLOCKS_HERE // KV_STEP

    def fetch(step):
        part = pl.ds(step * KV_STEP, KV_STEP)
        return pltpu.make_async_copy(kv_hbm.at[part], kv_ref.at[part], in_sems.at[step])

    asked = []
    for group in range(GROUPS):
        asked.append(pltpu.make_async_copy(q_hbm.at[group, pl.ds(0, ROWS_G)], q_ref.at[group], q_sems.at[group]))
        asked[-1].start()
    for step in range(steps):
        fetch(step).start()

    def clear(i, carry):
        acc_ref[pl.ds(pl.multiple_of(i * CAND, CAND), CAND), :] = jnp.zeros((CAND, DH), jnp.float32)
        return carry

    lax.fori_loop(0, REQUESTS, clear, 0, unroll=4)
    for copy in asked:
        copy.wait()

    def work(step, carry):
        fetch(step).wait()
        parts = []
        for u in range(KV_STEP):
            block = step * KV_STEP + u
            place = pos_ref[block]
            query = q_ref[place >> 2, pl.ds(pl.multiple_of((place & 3) * CAND, CAND), CAND), :]
            keys = kv_ref[block, :, :DH].astype(jnp.float32).T.astype(jnp.bfloat16)
            scores = jnp.dot(query, keys, preferred_element_type=jnp.float32)
            half = scores * (0.5 * DH ** (-0.5))
            silu = half + half * jnp.tanh(half)
            weights = jnp.concatenate(
                [
                    (silu[t * TILE : (t + 1) * TILE] * mask_ref[block * CT + t]).astype(jnp.bfloat16)
                    for t in range(CT)
                ],
                axis=0,
            )
            parts.append(jnp.dot(weights, kv_ref[block, :, DH:], preferred_element_type=jnp.float32))
        for u in range(KV_STEP):
            rows = pl.ds(pl.multiple_of(pos_ref[step * KV_STEP + u] * CAND, CAND), CAND)
            acc_ref[rows, :] += parts[u]
        return carry

    lax.fori_loop(0, steps, work, 0)

    core = core_ref[0]
    copies = []
    for out, (ref, hbm, side) in enumerate(((send_ref, send_hbm, 1 - core), (keep_ref, keep_hbm, core))):

        def split(target, carry):
            first = target * (CORES * PIECE) + side * PIECE
            for r in range(PIECE):
                ref[target, pl.ds(r * GROUPS, GROUPS), :] = acc_ref[
                    pl.ds(first + r, GROUPS, stride=ROWS_G), :
                ].astype(ref.dtype)
            return carry

        for z in range(0, ZS, 2):
            part = pl.ds(z * YS, 2 * YS)
            lax.fori_loop(z * YS, (z + 2) * YS, split, 0, unroll=4)
            copy = pltpu.make_async_copy(ref.at[part], hbm.at[part], out_sems.at[out * ZS + z])
            copy.start()
            copies.append(copy)
    for copy in copies:
        copy.wait()


def attend(positions, core, masks, payload, blocks):
    piece = jax.ShapeDtypeStruct((ZS * YS, GROUPS * PIECE, DH), jnp.bfloat16)
    smem, hbm = pl.BlockSpec(memory_space=pltpu.SMEM), pl.BlockSpec(memory_space=pltpu.HBM)
    return pl.pallas_call(
        attend_kernel,
        out_shape=(piece, piece),
        in_specs=[smem, smem, smem, hbm, hbm],
        out_specs=(hbm, hbm),
        scratch_shapes=[
            pltpu.VMEM((GROUPS, ROWS_G, DH), payload.dtype),
            pltpu.VMEM(blocks.shape, blocks.dtype),
            pltpu.VMEM((REQUESTS * CAND, DH), jnp.float32),
            pltpu.VMEM(piece.shape, piece.dtype),
            pltpu.VMEM(piece.shape, piece.dtype),
            pltpu.SemaphoreType.DMA((GROUPS,)),
            pltpu.SemaphoreType.DMA((BLOCKS_HERE // KV_STEP,)),
            pltpu.SemaphoreType.DMA((2 * ZS,)),
        ],
        compiler_params=pltpu.CompilerParams(vmem_limit_bytes=60 << 20),
        cost_estimate=pl.CostEstimate(
            flops=4 * BLOCKS_HERE * CAND * BLK * DH,
            bytes_accessed=10 << 20,
            transcendentals=BLOCKS_HERE * CAND * BLK,
        ),
    )(positions, core, masks, payload, blocks)


def finish_kernel(back_ref, gain_ref, gate_ref, token_ref, w_ref, out_ref):
    heads = []
    for head in range(H):
        total = back_ref[head * YS].astype(jnp.float32)
        for y in range(1, YS):
            total = total + back_ref[head * YS + y].astype(jnp.float32)
        heads.append(total.astype(jnp.bfloat16).astype(jnp.float32))
    rows = jnp.concatenate(heads, axis=1)
    centred = rows - jnp.mean(rows, axis=-1, keepdims=True)
    variance = jnp.mean(centred * centred, axis=-1, keepdims=True)
    normed = centred * lax.rsqrt(variance + EPS) * gain_ref[...]
    gate = gate_ref[...].astype(jnp.float32)
    gated = (normed * (gate * jax.nn.sigmoid(gate))).astype(jnp.bfloat16)
    projected = jnp.dot(gated, w_ref[...], preferred_element_type=jnp.float32)
    out_ref[...] = (token_ref[...].astype(jnp.float32) + projected).astype(out_ref.dtype)


def finish(back, gain, gate_rows, token_rows, w_all):
    return pl.pallas_call(
        finish_kernel,
        out_shape=jax.ShapeDtypeStruct(token_rows.shape, token_rows.dtype),
        in_specs=[pl.BlockSpec(memory_space=pltpu.VMEM)] * 5,
        out_specs=pl.BlockSpec(memory_space=pltpu.VMEM),
        compiler_params=pltpu.CompilerParams(vmem_limit_bytes=24 << 20),
    )(back, gain, gate_rows, token_rows, w_all)


def describe(cut, yc, hist_blocks, ranker_list, owner_ids, block_mask):
    owners = lax.dynamic_index_in_dim(owner_ids, cut, 0, keepdims=False).reshape(-1)
    ranking = lax.dynamic_index_in_dim(ranker_list, cut, 0, keepdims=False)
    lengths = lax.dynamic_index_in_dim(hist_blocks, cut, 0, keepdims=False)
    tiles = lax.dynamic_index_in_dim(block_mask, cut, 0, keepdims=False)
    source = jnp.arange(SOURCES, dtype=jnp.int32)
    source = (source // ZS) * (ZS * YS * CORES) + (source % ZS) * (YS * CORES) + yc
    found = owners[None, :] == source[:, None]
    place = jnp.arange(REQUESTS * HB, dtype=jnp.int32)[None, :]
    first = jnp.min(jnp.where(found, place, REQUESTS * HB - 1), axis=1)
    last = jnp.max(jnp.where(found, place, 0), axis=1)
    places = jnp.stack([first, last], axis=1).reshape(-1)
    request, block = places // HB, places % HB
    slots = jnp.arange(REQUESTS, dtype=jnp.int32)
    positions = jnp.sum(jnp.where(ranking[None, :] == request[:, None], slots[None, :], 0), axis=1)
    live = (block < lengths[request]).astype(jnp.float32)
    masks = tiles[request, :, block].astype(jnp.float32) * live[:, None]
    return positions, masks.reshape(-1)


def local(
    kv_cache,
    queries,
    gates,
    tokens,
    w_out,
    norm_gain,
    hist_blocks,
    ranker_list,
    owner_ids,
    slot_ids,
    block_mask,
):
    cut = lax.axis_index("cuts")
    core = lax.axis_index("core")
    me = lax.axis_index(("cuts", "z", "y", "core"))
    yc = lax.axis_index(("y", "core"))
    packed = pack(me, owner_ids, slot_ids, kv_cache)
    arrived = lax.all_to_all(packed, ("cuts", "z"), split_axis=0, concat_axis=0, tiled=True)
    payload = lax.all_gather(queries.reshape(ROWS_G, DH), ("y", "core"), axis=0, tiled=True)
    payload = payload.reshape(GROUPS, ROWS_G, DH)
    w_all = lax.all_gather(w_out, ("z", "y", "core"), axis=0, tiled=True)
    positions, masks = describe(cut, yc, hist_blocks, ranker_list, owner_ids, block_mask)
    keep, send = attend(
        positions, core.reshape(1), masks, payload, arrived.reshape(BLOCKS_HERE, BLK, SLAB)
    )
    other = lax.ppermute(send, "core", [(0, 1), (1, 0)])
    both = (keep.astype(jnp.float32) + other.astype(jnp.float32)).astype(jnp.bfloat16)
    both, w_all = lax.optimization_barrier((both, w_all))
    back = lax.all_to_all(both, ("z", "y"), split_axis=0, concat_axis=0, tiled=True)
    width = H * DH
    gate_rows = gates.reshape(GROUPS, PIECE, width).transpose(1, 0, 2).reshape(-1, width)
    token_rows = tokens.reshape(GROUPS, PIECE, width).transpose(1, 0, 2).reshape(-1, width)
    mixed = finish(back, norm_gain.reshape(1, width), gate_rows, token_rows, w_all)
    return mixed.reshape(PIECE, GROUPS, width).transpose(1, 0, 2).reshape(tokens.shape)


def solution(mesh):
    grid = Mesh(
        mesh.devices.reshape(CUTS, ZS, YS, CORES), ("cuts", "z", "y", "core")
    )
    dev = ("z", "y", "core")
    return jax.shard_map(
        local,
        mesh=grid,
        in_specs=(
            P(("cuts",) + dev, None, None),
            P("cuts", dev, None, None),
            P("cuts", None, dev, None),
            P("cuts", None, dev, None),
            P(dev, None),
            P(),
            P(),
            P(),
            P(),
            P(),
            P(),
        ),
        out_specs=P("cuts", None, dev, None),
        check_vma=False,
    )
```

```python
import jax
import jax.numpy as jnp
from jax import lax
from jax.experimental import pallas as pl
from jax.experimental.pallas import tpu as pltpu
from jax.sharding import Mesh, PartitionSpec as P

H = 8
DH = 128
HB = 32
RQ = 4
TILE = 32
BLK = 128
CUTS, ZS, YS, CORES = 4, 8, 8, 2
GROUPS = 16
REQUESTS = 64
CAND = 192
CT = 6
ROWS_G = RQ * CAND
OWN = 2
SLAB = 2 * DH
PIECE = 6
SOURCES = CUTS * ZS
BLOCKS_HERE = SOURCES * OWN
KV_STEP = 8
EPS = 1e-05
W_ROWS = 64
PAYLOAD = ROWS_G + W_ROWS


def pack_kernel(self_ref, owner_hbm, slot_hbm, kv_ref, out_ref, owner_ref, slot_ref, held, sems, in_sems, out_sems):
    me = self_ref[0]
    tables = [
        pltpu.make_async_copy(owner_hbm, owner_ref, sems.at[0]),
        pltpu.make_async_copy(slot_hbm, slot_ref, sems.at[1]),
    ]
    for table in tables:
        table.start()
    for table in tables:
        table.wait()
    blocks = lax.broadcasted_iota(jnp.int32, (HB, REQUESTS), 0)
    rows = lax.broadcasted_iota(jnp.int32, (HB, REQUESTS), 1)
    place = (rows * HB + blocks) * 8
    fetches = []
    for cut in range(CUTS):
        mine = owner_ref[cut] == me
        code = place + slot_ref[cut]
        first = jnp.min(jnp.where(mine, code, REQUESTS * HB * 8 - 1))
        last = jnp.max(jnp.where(mine, code, 0))
        for own, found in enumerate((first, last)):
            i = cut * OWN + own
            fetch = pltpu.make_async_copy(kv_ref.at[found & 7], held.at[i], in_sems.at[i])
            fetch.start()
            fetches.append(fetch)
    stores = []
    for i, fetch in enumerate(fetches):
        fetch.wait()
        for head in range(H):
            store = pltpu.make_async_copy(
                held.at[i, :, pl.ds(head * SLAB, SLAB)],
                out_ref.at[(i // OWN) * H + head, i % OWN],
                out_sems.at[i * H + head],
            )
            store.start()
            stores.append(store)
    for store in stores:
        store.wait()


def pack(me, owner_ids, slot_ids, kv_cache):
    count = CUTS * OWN
    owner_ids, slot_ids = owner_ids.transpose(0, 2, 1), slot_ids.transpose(0, 2, 1)
    return pl.pallas_call(
        pack_kernel,
        out_shape=jax.ShapeDtypeStruct((SOURCES, OWN, BLK, SLAB), kv_cache.dtype),
        in_specs=[
            pl.BlockSpec(memory_space=pltpu.SMEM),
            pl.BlockSpec(memory_space=pltpu.HBM),
            pl.BlockSpec(memory_space=pltpu.HBM),
            pl.BlockSpec(memory_space=pltpu.HBM),
        ],
        out_specs=pl.BlockSpec(memory_space=pltpu.HBM),
        scratch_shapes=[
            pltpu.VMEM(owner_ids.shape, jnp.int32),
            pltpu.VMEM(slot_ids.shape, jnp.int32),
            pltpu.VMEM((count, BLK, H * SLAB), kv_cache.dtype),
            pltpu.SemaphoreType.DMA((2,)),
            pltpu.SemaphoreType.DMA((count,)),
            pltpu.SemaphoreType.DMA((count * H,)),
        ],
        compiler_params=pltpu.CompilerParams(vmem_limit_bytes=60 << 20),
    )(me.reshape(1), owner_ids, slot_ids, kv_cache)


def attend_kernel(
    pos_ref, core_ref, mask_ref, q_hbm, kv_hbm, keep_hbm, send_hbm, q_ref, kv_ref, acc_ref, keep_ref, send_ref, q_sems, in_sems, out_sems
):
    steps = BLOCKS_HERE // KV_STEP

    def fetch(step):
        part = pl.ds(step * KV_STEP, KV_STEP)
        return pltpu.make_async_copy(kv_hbm.at[part], kv_ref.at[part], in_sems.at[step])

    asked = []
    for group in range(GROUPS):
        asked.append(pltpu.make_async_copy(q_hbm.at[group, pl.ds(0, ROWS_G)], q_ref.at[group], q_sems.at[group]))
        asked[-1].start()
    for step in range(steps):
        fetch(step).start()

    def clear(i, carry):
        acc_ref[pl.ds(pl.multiple_of(i * CAND, CAND), CAND), :] = jnp.zeros((CAND, DH), jnp.float32)
        return carry

    lax.fori_loop(0, REQUESTS, clear, 0, unroll=4)
    for copy in asked:
        copy.wait()

    def work(step, carry):
        fetch(step).wait()
        parts = []
        for u in range(KV_STEP):
            block = step * KV_STEP + u
            place = pos_ref[block]
            query = q_ref[place >> 2, pl.ds(pl.multiple_of((place & 3) * CAND, CAND), CAND), :]
            keys = kv_ref[block, :, :DH].astype(jnp.float32).T.astype(jnp.bfloat16)
            scores = jnp.dot(query, keys, preferred_element_type=jnp.float32)
            half = scores * (0.5 * DH ** (-0.5))
            silu = half + half * jnp.tanh(half)
            weights = jnp.concatenate(
                [
                    (silu[t * TILE : (t + 1) * TILE] * mask_ref[block * CT + t]).astype(jnp.bfloat16)
                    for t in range(CT)
                ],
                axis=0,
            )
            parts.append(jnp.dot(weights, kv_ref[block, :, DH:], preferred_element_type=jnp.float32))
        for u in range(KV_STEP):
            rows = pl.ds(pl.multiple_of(pos_ref[step * KV_STEP + u] * CAND, CAND), CAND)
            acc_ref[rows, :] += parts[u]
        return carry

    lax.fori_loop(0, steps, work, 0)

    core = core_ref[0]
    copies = []
    for out, (ref, hbm, side) in enumerate(((send_ref, send_hbm, 1 - core), (keep_ref, keep_hbm, core))):

        def split(target, carry):
            first = target * (CORES * PIECE) + side * PIECE
            for r in range(PIECE):
                ref[target, pl.ds(r * GROUPS, GROUPS), :] = acc_ref[
                    pl.ds(first + r, GROUPS, stride=ROWS_G), :
                ].astype(ref.dtype)
            return carry

        for z in range(0, ZS, 2):
            part = pl.ds(z * YS, 2 * YS)
            lax.fori_loop(z * YS, (z + 2) * YS, split, 0, unroll=4)
            copy = pltpu.make_async_copy(ref.at[part], hbm.at[part], out_sems.at[out * ZS + z])
            copy.start()
            copies.append(copy)
    for copy in copies:
        copy.wait()


def attend(positions, core, masks, payload, blocks):
    piece = jax.ShapeDtypeStruct((ZS * YS, GROUPS * PIECE, DH), jnp.bfloat16)
    smem, hbm = pl.BlockSpec(memory_space=pltpu.SMEM), pl.BlockSpec(memory_space=pltpu.HBM)
    return pl.pallas_call(
        attend_kernel,
        out_shape=(piece, piece),
        in_specs=[smem, smem, smem, hbm, hbm],
        out_specs=(hbm, hbm),
        scratch_shapes=[
            pltpu.VMEM((GROUPS, ROWS_G, DH), payload.dtype),
            pltpu.VMEM(blocks.shape, blocks.dtype),
            pltpu.VMEM((REQUESTS * CAND, DH), jnp.float32),
            pltpu.VMEM(piece.shape, piece.dtype),
            pltpu.VMEM(piece.shape, piece.dtype),
            pltpu.SemaphoreType.DMA((GROUPS,)),
            pltpu.SemaphoreType.DMA((BLOCKS_HERE // KV_STEP,)),
            pltpu.SemaphoreType.DMA((2 * ZS,)),
        ],
        compiler_params=pltpu.CompilerParams(vmem_limit_bytes=60 << 20),
        cost_estimate=pl.CostEstimate(
            flops=4 * BLOCKS_HERE * CAND * BLK * DH,
            bytes_accessed=10 << 20,
            transcendentals=BLOCKS_HERE * CAND * BLK,
        ),
    )(positions, core, masks, payload, blocks)


def finish_kernel(back_ref, gain_ref, gate_ref, token_ref, w_ref, out_ref):
    heads = []
    for head in range(H):
        total = back_ref[head * YS].astype(jnp.float32)
        for y in range(1, YS):
            total = total + back_ref[head * YS + y].astype(jnp.float32)
        heads.append(total.astype(jnp.bfloat16).astype(jnp.float32))
    rows = jnp.concatenate(heads, axis=1)
    centred = rows - jnp.mean(rows, axis=-1, keepdims=True)
    variance = jnp.mean(centred * centred, axis=-1, keepdims=True)
    normed = centred * lax.rsqrt(variance + EPS) * gain_ref[...]
    gate = gate_ref[...].astype(jnp.float32)
    gated = (normed * (gate * jax.nn.sigmoid(gate))).astype(jnp.bfloat16)
    projected = jnp.dot(gated, w_ref[...], preferred_element_type=jnp.float32)
    out_ref[...] = (token_ref[...].astype(jnp.float32) + projected).astype(out_ref.dtype)


def finish(back, gain, gate_rows, token_rows, w_all):
    return pl.pallas_call(
        finish_kernel,
        out_shape=jax.ShapeDtypeStruct(token_rows.shape, token_rows.dtype),
        in_specs=[pl.BlockSpec(memory_space=pltpu.VMEM)] * 5,
        out_specs=pl.BlockSpec(memory_space=pltpu.VMEM),
        compiler_params=pltpu.CompilerParams(vmem_limit_bytes=24 << 20),
    )(back, gain, gate_rows, token_rows, w_all)


def describe(cut, yc, hist_blocks, ranker_list, owner_ids, block_mask):
    owners = lax.dynamic_index_in_dim(owner_ids, cut, 0, keepdims=False).reshape(-1)
    ranking = lax.dynamic_index_in_dim(ranker_list, cut, 0, keepdims=False)
    lengths = lax.dynamic_index_in_dim(hist_blocks, cut, 0, keepdims=False)
    tiles = lax.dynamic_index_in_dim(block_mask, cut, 0, keepdims=False)
    source = jnp.arange(SOURCES, dtype=jnp.int32)
    source = (source // ZS) * (ZS * YS * CORES) + (source % ZS) * (YS * CORES) + yc
    found = owners[None, :] == source[:, None]
    place = jnp.arange(REQUESTS * HB, dtype=jnp.int32)[None, :]
    first = jnp.min(jnp.where(found, place, REQUESTS * HB - 1), axis=1)
    last = jnp.max(jnp.where(found, place, 0), axis=1)
    places = jnp.stack([first, last], axis=1).reshape(-1)
    request, block = places // HB, places % HB
    slots = jnp.arange(REQUESTS, dtype=jnp.int32)
    positions = jnp.sum(jnp.where(ranking[None, :] == request[:, None], slots[None, :], 0), axis=1)
    live = (block < lengths[request]).astype(jnp.float32)
    masks = tiles[request, :, block].astype(jnp.float32) * live[:, None]
    return positions, masks.reshape(-1)


def local(
    kv_cache,
    queries,
    gates,
    tokens,
    w_out,
    norm_gain,
    hist_blocks,
    ranker_list,
    owner_ids,
    slot_ids,
    block_mask,
):
    cut = lax.axis_index("cuts")
    core = lax.axis_index("core")
    me = lax.axis_index(("cuts", "z", "y", "core"))
    yc = lax.axis_index(("y", "core"))
    packed = pack(me, owner_ids, slot_ids, kv_cache)
    arrived = lax.all_to_all(packed, ("cuts", "z"), split_axis=0, concat_axis=0, tiled=True)
    payload = jnp.concatenate([queries.reshape(ROWS_G, DH), w_out.reshape(W_ROWS, DH)], axis=0)
    payload = lax.all_gather(payload, ("y", "core"), axis=0, tiled=True).reshape(GROUPS, PAYLOAD, DH)
    w_head = payload[:, ROWS_G:].reshape(DH, H * DH)
    w_all = lax.all_gather(w_head, "z", axis=0, tiled=True)
    positions, masks = describe(cut, yc, hist_blocks, ranker_list, owner_ids, block_mask)
    keep, send = attend(
        positions, core.reshape(1), masks, payload, arrived.reshape(BLOCKS_HERE, BLK, SLAB)
    )
    other = lax.ppermute(send, "core", [(0, 1), (1, 0)])
    both = (keep.astype(jnp.float32) + other.astype(jnp.float32)).astype(jnp.bfloat16)
    both, w_all = lax.optimization_barrier((both, w_all))
    back = lax.all_to_all(both, ("z", "y"), split_axis=0, concat_axis=0, tiled=True)
    width = H * DH
    gate_rows = gates.reshape(GROUPS, PIECE, width).transpose(1, 0, 2).reshape(-1, width)
    token_rows = tokens.reshape(GROUPS, PIECE, width).transpose(1, 0, 2).reshape(-1, width)
    mixed = finish(back, norm_gain.reshape(1, width), gate_rows, token_rows, w_all)
    return mixed.reshape(PIECE, GROUPS, width).transpose(1, 0, 2).reshape(tokens.shape)


def solution(mesh):
    grid = Mesh(
        mesh.devices.reshape(CUTS, ZS, YS, CORES), ("cuts", "z", "y", "core")
    )
    dev = ("z", "y", "core")
    return jax.shard_map(
        local,
        mesh=grid,
        in_specs=(
            P(("cuts",) + dev, None, None),
            P("cuts", dev, None, None),
            P("cuts", None, dev, None),
            P("cuts", None, dev, None),
            P(dev, None),
            P(),
            P(),
            P(),
            P(),
            P(),
            P(),
        ),
        out_specs=P("cuts", None, dev, None),
        check_vma=False,
    )
```

```python
import jax
import jax.numpy as jnp
from jax import lax
from jax.experimental import pallas as pl
from jax.experimental.pallas import tpu as pltpu
from jax.sharding import Mesh, PartitionSpec as P

H = 8
DH = 128
HB = 32
RQ = 4
TILE = 32
BLK = 128
CUTS, ZS, YS, CORES = 4, 8, 8, 2
GROUPS = 16
REQUESTS = 64
CAND = 192
CT = 6
ROWS_G = RQ * CAND
OWN = 2
SLAB = 2 * DH
PIECE = 6
SOURCES = CUTS * ZS
BLOCKS_HERE = SOURCES * OWN
KV_STEP = 8
EPS = 1e-05
W_ROWS = 64
PAYLOAD = ROWS_G + W_ROWS


def pack_kernel(self_ref, owner_hbm, slot_hbm, kv_ref, out_ref, owner_ref, slot_ref, held, sems, in_sems, out_sems):
    me = self_ref[0]
    tables = [
        pltpu.make_async_copy(owner_hbm, owner_ref, sems.at[0]),
        pltpu.make_async_copy(slot_hbm, slot_ref, sems.at[1]),
    ]
    for table in tables:
        table.start()
    for table in tables:
        table.wait()
    blocks = lax.broadcasted_iota(jnp.int32, (HB, REQUESTS), 0)
    rows = lax.broadcasted_iota(jnp.int32, (HB, REQUESTS), 1)
    place = (rows * HB + blocks) * 8
    fetches = []
    for cut in range(CUTS):
        mine = owner_ref[cut] == me
        code = place + slot_ref[cut]
        first = jnp.min(jnp.where(mine, code, REQUESTS * HB * 8 - 1))
        last = jnp.max(jnp.where(mine, code, 0))
        for own, found in enumerate((first, last)):
            i = cut * OWN + own
            fetch = pltpu.make_async_copy(kv_ref.at[found & 7], held.at[i], in_sems.at[i])
            fetch.start()
            fetches.append(fetch)
    stores = []
    for i, fetch in enumerate(fetches):
        fetch.wait()
        for head in range(H):
            store = pltpu.make_async_copy(
                held.at[i, :, pl.ds(head * SLAB, SLAB)],
                out_ref.at[(i // OWN) * H + head, i % OWN],
                out_sems.at[i * H + head],
            )
            store.start()
            stores.append(store)
    for store in stores:
        store.wait()


def pack(me, owner_ids, slot_ids, kv_cache):
    count = CUTS * OWN
    owner_ids, slot_ids = owner_ids.transpose(0, 2, 1), slot_ids.transpose(0, 2, 1)
    return pl.pallas_call(
        pack_kernel,
        out_shape=jax.ShapeDtypeStruct((SOURCES, OWN, BLK, SLAB), kv_cache.dtype),
        in_specs=[
            pl.BlockSpec(memory_space=pltpu.SMEM),
            pl.BlockSpec(memory_space=pltpu.HBM),
            pl.BlockSpec(memory_space=pltpu.HBM),
            pl.BlockSpec(memory_space=pltpu.HBM),
        ],
        out_specs=pl.BlockSpec(memory_space=pltpu.HBM),
        scratch_shapes=[
            pltpu.VMEM(owner_ids.shape, jnp.int32),
            pltpu.VMEM(slot_ids.shape, jnp.int32),
            pltpu.VMEM((count, BLK, H * SLAB), kv_cache.dtype),
            pltpu.SemaphoreType.DMA((2,)),
            pltpu.SemaphoreType.DMA((count,)),
            pltpu.SemaphoreType.DMA((count * H,)),
        ],
        compiler_params=pltpu.CompilerParams(vmem_limit_bytes=60 << 20),
    )(me.reshape(1), owner_ids, slot_ids, kv_cache)


def attend_kernel(
    pos_ref, core_ref, mask_ref, q_hbm, kv_hbm, keep_hbm, send_hbm, q_ref, kv_ref, acc_ref, keep_ref, send_ref, q_sems, in_sems, out_sems
):
    steps = BLOCKS_HERE // KV_STEP

    def fetch(step):
        part = pl.ds(step * KV_STEP, KV_STEP)
        return pltpu.make_async_copy(kv_hbm.at[part], kv_ref.at[part], in_sems.at[step])

    asked = []
    for group in range(GROUPS):
        asked.append(pltpu.make_async_copy(q_hbm.at[group, pl.ds(0, ROWS_G)], q_ref.at[group], q_sems.at[group]))
        asked[-1].start()
    for step in range(steps):
        fetch(step).start()

    def clear(i, carry):
        acc_ref[pl.ds(pl.multiple_of(i * CAND, CAND), CAND), :] = jnp.zeros((CAND, DH), jnp.float32)
        return carry

    lax.fori_loop(0, REQUESTS, clear, 0, unroll=4)
    for copy in asked:
        copy.wait()

    def work(step, carry):
        fetch(step).wait()
        parts = []
        for u in range(KV_STEP):
            block = step * KV_STEP + u
            place = pos_ref[block]
            query = q_ref[place >> 2, pl.ds(pl.multiple_of((place & 3) * CAND, CAND), CAND), :]
            keys = kv_ref[block, :, :DH].astype(jnp.float32).T.astype(jnp.bfloat16)
            scores = jnp.dot(query, keys, preferred_element_type=jnp.float32)
            half = scores * (0.5 * DH ** (-0.5))
            silu = half + half * jnp.tanh(half)
            weights = jnp.concatenate(
                [
                    (silu[t * TILE : (t + 1) * TILE] * mask_ref[block * CT + t]).astype(jnp.bfloat16)
                    for t in range(CT)
                ],
                axis=0,
            )
            parts.append(jnp.dot(weights, kv_ref[block, :, DH:], preferred_element_type=jnp.float32))
        for u in range(KV_STEP):
            rows = pl.ds(pl.multiple_of(pos_ref[step * KV_STEP + u] * CAND, CAND), CAND)
            acc_ref[rows, :] += parts[u]
        return carry

    lax.fori_loop(0, steps, work, 0)

    core = core_ref[0]
    copies = []
    for out, (ref, hbm, side) in enumerate(((send_ref, send_hbm, 1 - core), (keep_ref, keep_hbm, core))):

        def split(target, carry):
            first = target * (CORES * PIECE) + side * PIECE
            for r in range(PIECE):
                ref[target, pl.ds(r * GROUPS, GROUPS), :] = acc_ref[
                    pl.ds(first + r, GROUPS, stride=ROWS_G), :
                ].astype(ref.dtype)
            return carry

        for z in range(0, ZS, 2):
            part = pl.ds(z * YS, 2 * YS)
            lax.fori_loop(z * YS, (z + 2) * YS, split, 0, unroll=4)
            copy = pltpu.make_async_copy(ref.at[part], hbm.at[part], out_sems.at[out * ZS + z])
            copy.start()
            copies.append(copy)
    for copy in copies:
        copy.wait()


def attend(positions, core, masks, payload, blocks):
    piece = jax.ShapeDtypeStruct((ZS * YS, GROUPS * PIECE, DH), jnp.bfloat16)
    smem, hbm = pl.BlockSpec(memory_space=pltpu.SMEM), pl.BlockSpec(memory_space=pltpu.HBM)
    return pl.pallas_call(
        attend_kernel,
        out_shape=(piece, piece),
        in_specs=[smem, smem, smem, hbm, hbm],
        out_specs=(hbm, hbm),
        scratch_shapes=[
            pltpu.VMEM((GROUPS, ROWS_G, DH), payload.dtype),
            pltpu.VMEM(blocks.shape, blocks.dtype),
            pltpu.VMEM((REQUESTS * CAND, DH), jnp.float32),
            pltpu.VMEM(piece.shape, piece.dtype),
            pltpu.VMEM(piece.shape, piece.dtype),
            pltpu.SemaphoreType.DMA((GROUPS,)),
            pltpu.SemaphoreType.DMA((BLOCKS_HERE // KV_STEP,)),
            pltpu.SemaphoreType.DMA((2 * ZS,)),
        ],
        compiler_params=pltpu.CompilerParams(vmem_limit_bytes=60 << 20),
        cost_estimate=pl.CostEstimate(
            flops=4 * BLOCKS_HERE * CAND * BLK * DH,
            bytes_accessed=10 << 20,
            transcendentals=BLOCKS_HERE * CAND * BLK,
        ),
    )(positions, core, masks, payload, blocks)


def finish_kernel(back_ref, gain_ref, gate_ref, token_ref, w_ref, out_ref):
    heads = []
    for head in range(H):
        total = back_ref[head * YS].astype(jnp.float32)
        for y in range(1, YS):
            total = total + back_ref[head * YS + y].astype(jnp.float32)
        heads.append(total.astype(jnp.bfloat16).astype(jnp.float32))
    rows = jnp.concatenate(heads, axis=1)
    centred = rows - jnp.mean(rows, axis=-1, keepdims=True)
    variance = jnp.mean(centred * centred, axis=-1, keepdims=True)
    normed = centred * lax.rsqrt(variance + EPS) * gain_ref[...]
    gate = gate_ref[...].astype(jnp.float32)
    gated = (normed * (gate * jax.nn.sigmoid(gate))).astype(jnp.bfloat16)
    projected = jnp.dot(gated, w_ref[...], preferred_element_type=jnp.float32)
    out_ref[...] = (token_ref[...].astype(jnp.float32) + projected).astype(out_ref.dtype)


def finish(back, gain, gate_rows, token_rows, w_all):
    return pl.pallas_call(
        finish_kernel,
        out_shape=jax.ShapeDtypeStruct(token_rows.shape, token_rows.dtype),
        in_specs=[pl.BlockSpec(memory_space=pltpu.VMEM)] * 5,
        out_specs=pl.BlockSpec(memory_space=pltpu.VMEM),
        compiler_params=pltpu.CompilerParams(vmem_limit_bytes=24 << 20),
    )(back, gain, gate_rows, token_rows, w_all)


def describe(cut, yc, hist_blocks, ranker_list, owner_ids, block_mask):
    owners = lax.dynamic_index_in_dim(owner_ids, cut, 0, keepdims=False).reshape(-1)
    ranking = lax.dynamic_index_in_dim(ranker_list, cut, 0, keepdims=False)
    lengths = lax.dynamic_index_in_dim(hist_blocks, cut, 0, keepdims=False)
    tiles = lax.dynamic_index_in_dim(block_mask, cut, 0, keepdims=False)
    source = jnp.arange(SOURCES, dtype=jnp.int32)
    source = (source // ZS) * (ZS * YS * CORES) + (source % ZS) * (YS * CORES) + yc
    found = owners[None, :] == source[:, None]
    place = jnp.arange(REQUESTS * HB, dtype=jnp.int32)[None, :]
    first = jnp.min(jnp.where(found, place, REQUESTS * HB - 1), axis=1)
    last = jnp.max(jnp.where(found, place, 0), axis=1)
    places = jnp.stack([first, last], axis=1).reshape(-1)
    request, block = places // HB, places % HB
    slots = jnp.arange(REQUESTS, dtype=jnp.int32)
    positions = jnp.sum(jnp.where(ranking[None, :] == request[:, None], slots[None, :], 0), axis=1)
    live = (block < lengths[request]).astype(jnp.float32)
    masks = tiles[request, :, block].astype(jnp.float32) * live[:, None]
    return positions, masks.reshape(-1)


def local(
    kv_cache,
    queries,
    gates,
    tokens,
    w_out,
    norm_gain,
    hist_blocks,
    ranker_list,
    owner_ids,
    slot_ids,
    block_mask,
):
    cut = lax.axis_index("cuts")
    core = lax.axis_index("core")
    me = lax.axis_index(("cuts", "z", "y", "core"))
    yc = lax.axis_index(("y", "core"))
    packed = pack(me, owner_ids, slot_ids, kv_cache)
    arrived = lax.all_to_all(packed, ("cuts", "z"), split_axis=0, concat_axis=0, tiled=True)
    payload = jnp.concatenate([queries.reshape(ROWS_G, DH), w_out.reshape(W_ROWS, DH)], axis=0)
    payload = lax.all_gather(payload, ("y", "core"), axis=0, tiled=True).reshape(GROUPS, PAYLOAD, DH)
    w_head = lax.dynamic_slice_in_dim(payload[:, ROWS_G:], cut * (GROUPS // CUTS), GROUPS // CUTS)
    w_all = lax.all_gather(w_head.reshape(DH // CUTS, H * DH), ("z", "cuts"), axis=0, tiled=True)
    positions, masks = describe(cut, yc, hist_blocks, ranker_list, owner_ids, block_mask)
    keep, send = attend(
        positions, core.reshape(1), masks, payload, arrived.reshape(BLOCKS_HERE, BLK, SLAB)
    )
    other = lax.ppermute(send, "core", [(0, 1), (1, 0)])
    both = (keep.astype(jnp.float32) + other.astype(jnp.float32)).astype(jnp.bfloat16)
    both, w_all = lax.optimization_barrier((both, w_all))
    back = lax.all_to_all(both, ("z", "y"), split_axis=0, concat_axis=0, tiled=True)
    width = H * DH
    gate_rows = gates.reshape(GROUPS, PIECE, width).transpose(1, 0, 2).reshape(-1, width)
    token_rows = tokens.reshape(GROUPS, PIECE, width).transpose(1, 0, 2).reshape(-1, width)
    mixed = finish(back, norm_gain.reshape(1, width), gate_rows, token_rows, w_all)
    return mixed.reshape(PIECE, GROUPS, width).transpose(1, 0, 2).reshape(tokens.shape)


def solution(mesh):
    grid = Mesh(
        mesh.devices.reshape(CUTS, ZS, YS, CORES), ("cuts", "z", "y", "core")
    )
    dev = ("z", "y", "core")
    return jax.shard_map(
        local,
        mesh=grid,
        in_specs=(
            P(("cuts",) + dev, None, None),
            P("cuts", dev, None, None),
            P("cuts", None, dev, None),
            P("cuts", None, dev, None),
            P(dev, None),
            P(),
            P(),
            P(),
            P(),
            P(),
            P(),
        ),
        out_specs=P("cuts", None, dev, None),
        check_vma=False,
    )
```

```python
import jax
import jax.numpy as jnp
from jax import lax
from jax.experimental import pallas as pl
from jax.experimental.pallas import tpu as pltpu
from jax.sharding import Mesh, PartitionSpec as P

H = 8
DH = 128
HB = 32
RQ = 4
TILE = 32
BLK = 128
CUTS, ZS, YS, CORES = 4, 8, 8, 2
GROUPS = 16
REQUESTS = 64
CAND = 192
CT = 6
ROWS_G = RQ * CAND
OWN = 2
SLAB = 2 * DH
PIECE = 6
SOURCES = CUTS * ZS
BLOCKS_HERE = SOURCES * OWN
KV_STEP = 8
EPS = 1e-05
W_ROWS = 64
PAYLOAD = ROWS_G + W_ROWS


def pack_kernel(self_ref, owner_hbm, slot_hbm, kv_ref, out_ref, owner_ref, slot_ref, held, sems, in_sems, out_sems):
    me = self_ref[0]
    tables = [
        pltpu.make_async_copy(owner_hbm, owner_ref, sems.at[0]),
        pltpu.make_async_copy(slot_hbm, slot_ref, sems.at[1]),
    ]
    for table in tables:
        table.start()
    for table in tables:
        table.wait()
    blocks = lax.broadcasted_iota(jnp.int32, (HB, REQUESTS), 0)
    rows = lax.broadcasted_iota(jnp.int32, (HB, REQUESTS), 1)
    place = (rows * HB + blocks) * 8
    fetches = []
    for cut in range(CUTS):
        mine = owner_ref[cut] == me
        code = place + slot_ref[cut]
        first = jnp.min(jnp.where(mine, code, REQUESTS * HB * 8 - 1))
        last = jnp.max(jnp.where(mine, code, 0))
        for own, found in enumerate((first, last)):
            i = cut * OWN + own
            fetch = pltpu.make_async_copy(kv_ref.at[found & 7], held.at[i], in_sems.at[i])
            fetch.start()
            fetches.append(fetch)
    stores = []
    for i, fetch in enumerate(fetches):
        fetch.wait()
        for head in range(H):
            store = pltpu.make_async_copy(
                held.at[i, :, pl.ds(head * SLAB, SLAB)],
                out_ref.at[(i // OWN) * H + head, i % OWN],
                out_sems.at[i * H + head],
            )
            store.start()
            stores.append(store)
    for store in stores:
        store.wait()


def pack(me, owner_ids, slot_ids, kv_cache):
    count = CUTS * OWN
    owner_ids, slot_ids = owner_ids.transpose(0, 2, 1), slot_ids.transpose(0, 2, 1)
    return pl.pallas_call(
        pack_kernel,
        out_shape=jax.ShapeDtypeStruct((SOURCES, OWN, BLK, SLAB), kv_cache.dtype),
        in_specs=[
            pl.BlockSpec(memory_space=pltpu.SMEM),
            pl.BlockSpec(memory_space=pltpu.HBM),
            pl.BlockSpec(memory_space=pltpu.HBM),
            pl.BlockSpec(memory_space=pltpu.HBM),
        ],
        out_specs=pl.BlockSpec(memory_space=pltpu.HBM),
        scratch_shapes=[
            pltpu.VMEM(owner_ids.shape, jnp.int32),
            pltpu.VMEM(slot_ids.shape, jnp.int32),
            pltpu.VMEM((count, BLK, H * SLAB), kv_cache.dtype),
            pltpu.SemaphoreType.DMA((2,)),
            pltpu.SemaphoreType.DMA((count,)),
            pltpu.SemaphoreType.DMA((count * H,)),
        ],
        compiler_params=pltpu.CompilerParams(vmem_limit_bytes=60 << 20),
    )(me.reshape(1), owner_ids, slot_ids, kv_cache)


def attend_kernel(
    pos_ref, core_ref, mask_ref, q_hbm, kv_hbm, keep_hbm, send_hbm, q_ref, kv_ref, acc_ref, keep_ref, send_ref, q_sems, in_sems, out_sems
):
    steps = BLOCKS_HERE // KV_STEP

    def fetch(step):
        part = pl.ds(step * KV_STEP, KV_STEP)
        return pltpu.make_async_copy(kv_hbm.at[part], kv_ref.at[part], in_sems.at[step])

    asked = []
    for group in range(GROUPS):
        asked.append(pltpu.make_async_copy(q_hbm.at[group, pl.ds(0, ROWS_G)], q_ref.at[group], q_sems.at[group]))
        asked[-1].start()
    for step in range(steps):
        fetch(step).start()

    def clear(i, carry):
        acc_ref[pl.ds(pl.multiple_of(i * CAND, CAND), CAND), :] = jnp.zeros((CAND, DH), jnp.float32)
        return carry

    lax.fori_loop(0, REQUESTS, clear, 0, unroll=4)
    for copy in asked:
        copy.wait()

    def work(step, carry):
        fetch(step).wait()
        parts = []
        for u in range(KV_STEP):
            block = step * KV_STEP + u
            place = pos_ref[block]
            query = q_ref[place >> 2, pl.ds(pl.multiple_of((place & 3) * CAND, CAND), CAND), :]
            keys = kv_ref[block, :, :DH].astype(jnp.float32).T.astype(jnp.bfloat16)
            scores = jnp.dot(query, keys, preferred_element_type=jnp.float32)
            half = scores * (0.5 * DH ** (-0.5))
            silu = half + half * jnp.tanh(half)
            weights = jnp.concatenate(
                [
                    (silu[t * TILE : (t + 1) * TILE] * mask_ref[block * CT + t]).astype(jnp.bfloat16)
                    for t in range(CT)
                ],
                axis=0,
            )
            parts.append(jnp.dot(weights, kv_ref[block, :, DH:], preferred_element_type=jnp.float32))
        for u in range(KV_STEP):
            rows = pl.ds(pl.multiple_of(pos_ref[step * KV_STEP + u] * CAND, CAND), CAND)
            acc_ref[rows, :] += parts[u]
        return carry

    lax.fori_loop(0, steps, work, 0)

    core = core_ref[0]
    copies = []
    for out, (ref, hbm, side) in enumerate(((send_ref, send_hbm, 1 - core), (keep_ref, keep_hbm, core))):

        def split(target, carry):
            first = target * (CORES * PIECE) + side * PIECE
            for r in range(PIECE):
                ref[target, pl.ds(r * GROUPS, GROUPS), :] = acc_ref[
                    pl.ds(first + r, GROUPS, stride=ROWS_G), :
                ].astype(ref.dtype)
            return carry

        for z in range(0, ZS, 2):
            part = pl.ds(z * YS, 2 * YS)
            lax.fori_loop(z * YS, (z + 2) * YS, split, 0, unroll=4)
            copy = pltpu.make_async_copy(ref.at[part], hbm.at[part], out_sems.at[out * ZS + z])
            copy.start()
            copies.append(copy)
    for copy in copies:
        copy.wait()


def attend(positions, core, masks, payload, blocks):
    piece = jax.ShapeDtypeStruct((ZS * YS, GROUPS * PIECE, DH), jnp.bfloat16)
    smem, hbm = pl.BlockSpec(memory_space=pltpu.SMEM), pl.BlockSpec(memory_space=pltpu.HBM)
    return pl.pallas_call(
        attend_kernel,
        out_shape=(piece, piece),
        in_specs=[smem, smem, smem, hbm, hbm],
        out_specs=(hbm, hbm),
        scratch_shapes=[
            pltpu.VMEM((GROUPS, ROWS_G, DH), payload.dtype),
            pltpu.VMEM(blocks.shape, blocks.dtype),
            pltpu.VMEM((REQUESTS * CAND, DH), jnp.float32),
            pltpu.VMEM(piece.shape, piece.dtype),
            pltpu.VMEM(piece.shape, piece.dtype),
            pltpu.SemaphoreType.DMA((GROUPS,)),
            pltpu.SemaphoreType.DMA((BLOCKS_HERE // KV_STEP,)),
            pltpu.SemaphoreType.DMA((2 * ZS,)),
        ],
        compiler_params=pltpu.CompilerParams(vmem_limit_bytes=60 << 20),
        cost_estimate=pl.CostEstimate(
            flops=4 * BLOCKS_HERE * CAND * BLK * DH,
            bytes_accessed=10 << 20,
            transcendentals=BLOCKS_HERE * CAND * BLK,
        ),
    )(positions, core, masks, payload, blocks)


def finish_kernel(back_ref, gain_ref, gate_ref, token_ref, w_ref, out_ref):
    heads = []
    for head in range(H):
        total = back_ref[head * YS].astype(jnp.float32)
        for y in range(1, YS):
            total = total + back_ref[head * YS + y].astype(jnp.float32)
        heads.append(total.astype(jnp.bfloat16).astype(jnp.float32))
    rows = jnp.concatenate(heads, axis=1)
    centred = rows - jnp.mean(rows, axis=-1, keepdims=True)
    variance = jnp.mean(centred * centred, axis=-1, keepdims=True)
    normed = centred * lax.rsqrt(variance + EPS) * gain_ref[...]
    gate = gate_ref[...].astype(jnp.float32)
    gated = (normed * (gate * jax.nn.sigmoid(gate))).astype(jnp.bfloat16)
    projected = jnp.dot(gated, w_ref[...], preferred_element_type=jnp.float32)
    out_ref[...] = (token_ref[...].astype(jnp.float32) + projected).astype(out_ref.dtype)


def finish(back, gain, gate_rows, token_rows, w_all):
    return pl.pallas_call(
        finish_kernel,
        out_shape=jax.ShapeDtypeStruct(token_rows.shape, token_rows.dtype),
        in_specs=[pl.BlockSpec(memory_space=pltpu.VMEM)] * 5,
        out_specs=pl.BlockSpec(memory_space=pltpu.VMEM),
        compiler_params=pltpu.CompilerParams(vmem_limit_bytes=24 << 20),
    )(back, gain, gate_rows, token_rows, w_all)


def describe(cut, yc, hist_blocks, ranker_list, owner_ids, block_mask):
    owners = lax.dynamic_index_in_dim(owner_ids, cut, 0, keepdims=False).reshape(-1)
    ranking = lax.dynamic_index_in_dim(ranker_list, cut, 0, keepdims=False)
    lengths = lax.dynamic_index_in_dim(hist_blocks, cut, 0, keepdims=False)
    tiles = lax.dynamic_index_in_dim(block_mask, cut, 0, keepdims=False)
    source = jnp.arange(SOURCES, dtype=jnp.int32)
    source = (source // ZS) * (ZS * YS * CORES) + (source % ZS) * (YS * CORES) + yc
    found = owners[None, :] == source[:, None]
    place = jnp.arange(REQUESTS * HB, dtype=jnp.int32)[None, :]
    first = jnp.min(jnp.where(found, place, REQUESTS * HB - 1), axis=1)
    last = jnp.max(jnp.where(found, place, 0), axis=1)
    places = jnp.stack([first, last], axis=1).reshape(-1)
    request, block = places // HB, places % HB
    slots = jnp.arange(REQUESTS, dtype=jnp.int32)
    positions = jnp.sum(jnp.where(ranking[None, :] == request[:, None], slots[None, :], 0), axis=1)
    live = (block < lengths[request]).astype(jnp.float32)
    masks = tiles[request, :, block].astype(jnp.float32) * live[:, None]
    return positions, masks.reshape(-1)


def local(
    kv_cache,
    queries,
    gates,
    tokens,
    w_out,
    norm_gain,
    hist_blocks,
    ranker_list,
    owner_ids,
    slot_ids,
    block_mask,
):
    cut = lax.axis_index("cuts")
    core = lax.axis_index("core")
    me = lax.axis_index(("cuts", "z", "y", "core"))
    yc = lax.axis_index(("y", "core"))
    packed = pack(me, owner_ids, slot_ids, kv_cache)
    arrived = lax.all_to_all(packed, ("cuts", "z"), split_axis=0, concat_axis=0, tiled=True)
    payload = jnp.concatenate([queries.reshape(ROWS_G, DH), w_out.reshape(W_ROWS, DH)], axis=0)
    payload = lax.all_gather(payload, ("y", "core"), axis=0, tiled=True).reshape(GROUPS, PAYLOAD, DH)
    half = lax.dynamic_slice_in_dim(payload[:, ROWS_G:], core * (GROUPS // CORES), GROUPS // CORES)
    half = lax.all_gather(half.reshape(1, DH // CORES, H * DH), "z", axis=0, tiled=True)
    swapped = lax.ppermute(half, "core", [(0, 1), (1, 0)])
    w_all = jnp.stack(
        [jnp.where(core == 0, half, swapped), jnp.where(core == 0, swapped, half)], axis=1
    ).reshape(H * DH, H * DH)
    positions, masks = describe(cut, yc, hist_blocks, ranker_list, owner_ids, block_mask)
    arrived, w_all = lax.optimization_barrier((arrived, w_all))
    keep, send = attend(
        positions, core.reshape(1), masks, payload, arrived.reshape(BLOCKS_HERE, BLK, SLAB)
    )
    other = lax.ppermute(send, "core", [(0, 1), (1, 0)])
    both = (keep.astype(jnp.float32) + other.astype(jnp.float32)).astype(jnp.bfloat16)
    back = lax.all_to_all(both, ("z", "y"), split_axis=0, concat_axis=0, tiled=True)
    width = H * DH
    gate_rows = gates.reshape(GROUPS, PIECE, width).transpose(1, 0, 2).reshape(-1, width)
    token_rows = tokens.reshape(GROUPS, PIECE, width).transpose(1, 0, 2).reshape(-1, width)
    mixed = finish(back, norm_gain.reshape(1, width), gate_rows, token_rows, w_all)
    return mixed.reshape(PIECE, GROUPS, width).transpose(1, 0, 2).reshape(tokens.shape)


def solution(mesh):
    grid = Mesh(
        mesh.devices.reshape(CUTS, ZS, YS, CORES), ("cuts", "z", "y", "core")
    )
    dev = ("z", "y", "core")
    return jax.shard_map(
        local,
        mesh=grid,
        in_specs=(
            P(("cuts",) + dev, None, None),
            P("cuts", dev, None, None),
            P("cuts", None, dev, None),
            P("cuts", None, dev, None),
            P(dev, None),
            P(),
            P(),
            P(),
            P(),
            P(),
            P(),
        ),
        out_specs=P("cuts", None, dev, None),
        check_vma=False,
    )
```
